256 devices in a mesh: sec: 4 (over z_hi, core), op: 64 (over z_lo, y, x).
Axes of the slice: x: 4, y: 4, z: 8 (z_hi: 2, z_lo: 4; z = z_hi * 4 + z_lo), core: 2. Of those that a mesh axis runs over, the one named last changes fastest.
Arguments:
- wave_in: float32 [4, 4, 256, 256], P('sec'), may hold values from -6 to 6
- kept_states: int32 [4, 4], P('sec'), may hold values from 64 to 256, as said below
- left_ops: bfloat16 [4, 512, 4, 256, 256], P('sec', 'op')
- right_ops: bfloat16 [4, 512, 4, 256, 256], P('sec', 'op'), may hold values from -0.375 to 0.375
Outputs:
- wave_out: float32 [4, 4, 256, 256], P('sec')
- boundary: float32 [4, 4, 256, 256], P('sec')
The draws below stay inside these ranges and needn't reach their ends.
Inputs may be any that keep to these rules, and one draw needn't show every extreme that they name: `kept_states`: the first sector of every section keeps all 256 states.
All inputs are finite; a program needn't handle non-finite values.
Results may differ from the reference program's by a relative error of at most 0.0058.
Values sent between devices are 32-bit elements; how exact they have to be, the bound alone decides.
No kernel may reach another device: no remote copies, remote signals or barrier semaphores. Data moves between devices by JAX's collectives and lax.ppermute only.
A program may use at most 64 MiB of HBM per device.

```python
import math
import jax
import jax.numpy as jnp
from jax import lax

BLK = 256
SECT = 4
SECTIONS = 4
TERMS = 512


def draw_kept_states(key, part):
    key = jax.random.fold_in(key, 7)
    counts = jax.random.randint(key, (SECTIONS, SECT), BLK // 4, BLK + 1)
    return counts.at[:, 0].set(BLK).astype(jnp.int32)


def draw_left_ops(key, part):
    key = jax.random.fold_in(key, 11)
    shape = (SECTIONS, TERMS, SECT, BLK, BLK)
    rows = (jnp.arange(SECT * BLK, dtype=jnp.float32) / (SECT * BLK - 1)).reshape(SECT, BLK)
    base = jax.random.normal(key, shape, jnp.float32)
    scale = 3.0 ** rows
    values = base * scale[:, :, None] / jnp.sqrt(jnp.float32(BLK * TERMS))
    return values.astype(jnp.bfloat16)


def shard_levels(stream_key, extent, pieces, smallest, top_value):
    def one(position, blocks):
        draws = jax.random.uniform(jax.random.fold_in(jax.random.fold_in(stream_key, 6), position), (blocks,), jnp.float32, smallest / len(pieces), top_value / len(pieces))
        return jnp.repeat(jnp.exp(draws), extent[position] // blocks).reshape((-1,) + (1,) * (len(extent) - position - 1))

    factor_of = one(*pieces[0])
    for cut in pieces[1:]:
        factor_of = factor_of * one(*cut)
    return factor_of


def scatter_about(key, dims, deviation, bound, pieces=(), kind=jnp.bfloat16):
    loudness = shard_levels(key, dims, pieces, -0.22, 0.18) if pieces else 1.0
    entries = jax.random.normal(key, dims, jnp.float32) * deviation * loudness
    return jnp.minimum(jnp.maximum(entries, -bound), bound).astype(kind)


def setup_inputs(seed: int = 0) -> dict:
    keys = jax.random.split(jax.random.key(seed), 5)
    wave_in = scatter_about(keys[0], (SECTIONS, SECT, BLK, BLK), 1.0, 6.0, ((0, 4),), jnp.float32)
    kept_states = draw_kept_states(jax.random.fold_in(keys[4], 71), 0)
    left_ops = draw_left_ops(jax.random.fold_in(keys[4], 71), 0)
    right_ops = scatter_about(keys[3], (SECTIONS, TERMS, SECT, BLK, BLK), BLK ** -0.5, 0.375, ((0, 4), (1, 64)))
    return dict(wave_in=wave_in, kept_states=kept_states, left_ops=left_ops, right_ops=right_ops)


EPS = 1e-06
STEP_COEF = 0.5

def kept_mask(kept):
    cols = jnp.arange(BLK, dtype=jnp.int32)
    return (cols[None, :] < kept[:, None]).astype(jnp.float32)[:, None, :]

def davidson_update(state, sigma, mask):
    pp = jnp.sum(state * state)
    ps = jnp.sum(state * sigma)
    theta = ps / (pp + EPS)
    trial = mask * ((1.0 + STEP_COEF * theta) * state - STEP_COEF * sigma)
    scale = lax.rsqrt(jnp.mean(trial * trial) + EPS)
    return trial * scale

def section_steps(wave, left, right, kept):
    mask = kept_mask(kept)
    state = wave * mask
    for step in range(2):
        state_b = state.astype(jnp.bfloat16)

        def add_term(total, ops):
            left_one, right_one = ops
            mixed = jnp.einsum('sij,sjl->sil', state_b.astype(jnp.float32), right_one.astype(jnp.float32)).astype(jnp.bfloat16)
            return (total + jnp.einsum('sij,sjl->sil', left_one.astype(jnp.float32), mixed.astype(jnp.float32)), None)
        sigma, unused = lax.scan(add_term, jnp.zeros((SECT, BLK, BLK), jnp.float32), (left, right))
        state = davidson_update(state, sigma, mask)
    return state

def reference(wave_in, kept_states, left_ops, right_ops):
    states = []
    for index in range(SECTIONS):
        states.append(section_steps(wave_in[index], left_ops[index], right_ops[index], kept_states[index]))
    wave_out = jnp.stack(states)
    bounds = []
    for index in range(SECTIONS):
        partner = wave_out[index ^ 1] + wave_out[(index - 1) % SECTIONS]
        prod = jnp.einsum('sji,sjl->sil', wave_out[index], partner, precision=lax.Precision.HIGHEST)
        bounds.append(prod / math.sqrt(BLK))
    return (wave_out, jnp.stack(bounds))
```

```python
import math

import jax
import jax.numpy as jnp
from jax import lax
from jax.sharding import Mesh, PartitionSpec as P

EPS = 1e-06
STEP_COEF = 0.5
SEC = ("zh", "core")
OP = ("z", "y", "x")
PLANE = ("y", "x")


def paired(value, axis, apart):
    count = lax.axis_size(axis)
    return lax.ppermute(value, axis, [(i, i ^ apart) for i in range(count)])


def summed(partial):
    rows, width = partial.shape
    ways = lax.axis_size(PLANE)
    piece = lax.all_to_all(partial.reshape(ways, rows // ways, width), PLANE, 0, 0).sum(0)
    near = paired(piece, "z", 1)
    far = paired(piece, "z", 2)
    corner = paired(piece, "z", 3)
    piece = (piece + near) + (far + corner)
    copies = jnp.broadcast_to(piece[None], (ways,) + piece.shape)
    return lax.all_to_all(copies, PLANE, 0, 0).reshape(rows, width)


def shards(wave_in, kept_states, left_ops, right_ops):
    sectors, width = (wave_in.shape[1], wave_in.shape[2])
    cols = jnp.arange(width, dtype=jnp.int32)
    mask = (cols[None, :] < kept_states[0][:, None]).astype(jnp.float32)[:, None, :]
    state = wave_in[0] * mask
    left = left_ops[0]
    right = right_ops[0]
    for step in range(2):
        mixed = jnp.einsum(
            "sij,ksjl->ksil", state.astype(jnp.bfloat16), right, preferred_element_type=jnp.float32
        ).astype(jnp.bfloat16)
        partial_sigma = jnp.einsum("ksij,ksjl->sil", left, mixed, preferred_element_type=jnp.float32)
        sigma = summed(partial_sigma.reshape(sectors * width, width)).reshape(state.shape)
        pp = jnp.sum(state * state)
        ps = jnp.sum(state * sigma)
        theta = ps / (pp + EPS)
        trial = mask * ((1.0 + STEP_COEF * theta) * state - STEP_COEF * sigma)
        state = trial * lax.rsqrt(jnp.mean(trial * trial) + EPS)
    even_state = lax.ppermute(state, "core", [(0, 1), (1, 0)])
    odd_state = lax.ppermute(state, SEC, [(i, (i + 1) % 4) for i in range(4)])
    partner = even_state + odd_state
    bound = jnp.einsum("sji,sjl->sil", state, partner, precision=lax.Precision.HIGHEST) / math.sqrt(width)
    return (state[None], bound[None])


def solution(mesh):
    split = Mesh(mesh.devices.reshape(2, 2, 4, 4, 4), SEC + OP)
    return jax.shard_map(
        shards,
        mesh=split,
        in_specs=(
            P(SEC, None, None, None),
            P(SEC, None),
            P(SEC, OP, None, None, None),
            P(SEC, OP, None, None, None),
        ),
        out_specs=(P(SEC, None, None, None), P(SEC, None, None, None)),
        check_vma=False,
    )
```

```python
import functools
import math

import jax
import jax.numpy as jnp
from jax import lax
from jax.experimental import pallas as pl
from jax.experimental.pallas import tpu as pltpu
from jax.sharding import Mesh, PartitionSpec as P

EPS = 1e-06
STEP_COEF = 0.5
SEC = ("zh", "core")
OP = ("z1", "z0", "y", "x")
NEAR = ("z0", "y", "x")
SWAP = [(0, 1), (1, 0)]
VMEM_LIMIT = 24 * 2**20
CHUNK = 32


def mirrored():
    pairs = []
    for z in range(8):
        far = 7 - z
        pairs.append(((z // 4 * 2 + 1) * 4 + z % 4, (far // 4 * 2) * 4 + far % 4))
    return pairs


def masked(block, kept):
    cols = lax.broadcasted_iota(jnp.int32, block.shape, block.ndim - 1)
    return jnp.where(cols < kept, block, 0.0)


def folded(block):
    return block.reshape(-1, 8, block.shape[-1]).sum(0)


def chunk(i):
    return pl.ds(pl.multiple_of(i * CHUNK, CHUNK), CHUNK)


def update(rows, width, read_state, read_sigma, out_ref):
    count = rows // CHUNK
    zero = jnp.zeros((8, width), jnp.float32)

    def products(i, sums):
        state = read_state(i)
        return sums[0] + folded(state * state), sums[1] + folded(state * read_sigma(i))

    pp, ps = lax.fori_loop(0, count, products, (zero, zero), unroll=4)
    theta = jnp.sum(ps) / (jnp.sum(pp) + EPS)

    def trials(i, total):
        trial = (1.0 + STEP_COEF * theta) * read_state(i) - STEP_COEF * read_sigma(i)
        out_ref[chunk(i), :] = trial
        return total + folded(trial * trial)

    tt = lax.fori_loop(0, count, trials, zero, unroll=4)
    scale = lax.rsqrt(jnp.sum(tt) / (rows * width) + EPS)

    def scaled(i, carry):
        out_ref[chunk(i), :] = out_ref[chunk(i), :] * scale
        return carry

    lax.fori_loop(0, count, scaled, 0, unroll=4)


def sector_sums(state, left_ref, right_ref, s):
    terms = left_ref.shape[0]
    right = jnp.concatenate([right_ref[k, s] for k in range(terms)], axis=1)
    mixed = jnp.dot(state.astype(jnp.bfloat16), right, preferred_element_type=jnp.float32).astype(jnp.bfloat16)
    width = state.shape[1]
    mixed = jnp.concatenate([mixed[:, k * width : (k + 1) * width] for k in range(terms)], axis=0)
    left = jnp.concatenate([left_ref[k, s] for k in range(terms)], axis=1)
    return jnp.dot(left, mixed, preferred_element_type=jnp.float32)


def fetch(copies):
    started = []
    for s, (pairs, sems) in enumerate(copies):
        started.append([pltpu.make_async_copy(source, target, sems.at[j]) for j, (source, target) in enumerate(pairs)])
        for copy in started[s]:
            copy.start()
    return started


def first_kernel(kept_ref, wave_hbm, left_hbm, right_hbm, out_ref, left_ref, right_ref, wave_ref, sems):
    sectors, width = kept_ref.shape[1], wave_ref.shape[1]
    parts = [pl.ds(s * width, width) for s in range(sectors)]
    copies = fetch(
        [
            (
                [
                    (wave_hbm.at[parts[s]], wave_ref.at[parts[s]]),
                    (right_hbm.at[:, s], right_ref.at[:, s]),
                    (left_hbm.at[:, s], left_ref.at[:, s]),
                ],
                sems.at[s],
            )
            for s in range(sectors)
        ]
    )
    for s in range(sectors):
        for copy in copies[s]:
            copy.wait()
        out_ref[parts[s], :] = sector_sums(masked(wave_ref[parts[s], :], kept_ref[0, s]), left_ref, right_ref, s)


def second_kernel(kept_ref, wave_ref, sigma_ref, left_hbm, right_hbm, out_ref, state_ref, left_ref, right_ref, sems):
    sectors = kept_ref.shape[1]
    rows, width = wave_ref.shape
    share = rows // CHUNK // sectors
    copies = fetch(
        [
            (
                [(right_hbm.at[:, s], right_ref.at[:, s]), (left_hbm.at[:, s], left_ref.at[:, s])],
                sems.at[s],
            )
            for s in range(sectors)
        ]
    )
    update(
        rows,
        width,
        lambda i: masked(wave_ref[chunk(i), :], kept_ref[0, i // share]),
        lambda i: sigma_ref[chunk(i), :],
        state_ref,
    )
    for s in range(sectors):
        part = pl.ds(s * width, width)
        for copy in copies[s]:
            copy.wait()
        out_ref[part, :] = sector_sums(state_ref[part, :], left_ref, right_ref, s)


def own_kernel(state_ref, sigma_ref, out_ref):
    rows, width = state_ref.shape
    update(rows, width, lambda i: state_ref[chunk(i), :], lambda i: sigma_ref[chunk(i), :], out_ref)


def bound_kernel(sectors, core_ref, wave_ref, near_ref, far_ref, out_ref):
    width = wave_ref.shape[1]
    even = core_ref[0, 0] == 0
    for s in range(sectors):
        rows = pl.ds(s * width, width)
        near = near_ref[rows, :]
        partner = near + jnp.where(even, far_ref[rows, :], near)
        out_ref[rows, :] = lax.dot_general(
            wave_ref[rows, :],
            partner,
            (((0,), (0,)), ((), ())),
            precision=lax.Precision.HIGHEST,
            preferred_element_type=jnp.float32,
        ) / math.sqrt(width)


def params():
    return pltpu.CompilerParams(vmem_limit_bytes=VMEM_LIMIT)


def cost(flops, transfer):
    return pl.CostEstimate(flops=flops, bytes_accessed=transfer, transcendentals=0)


def smem():
    return pl.BlockSpec(memory_space=pltpu.SMEM)


def vmem():
    return pl.BlockSpec(memory_space=pltpu.VMEM)


def hbm():
    return pl.BlockSpec(memory_space=pltpu.HBM)


def in_hbm(*arrays):
    return [pltpu.with_memory_space_constraint(array, pltpu.HBM) for array in arrays]


def first_sums(kept, wave, left, right):
    terms, sectors, width, _ = left.shape
    return pl.pallas_call(
        first_kernel,
        in_specs=[smem()] + [hbm()] * 3,
        out_specs=vmem(),
        out_shape=jax.ShapeDtypeStruct(wave.shape, jnp.float32),
        scratch_shapes=[
            pltpu.VMEM(left.shape, left.dtype),
            pltpu.VMEM(right.shape, right.dtype),
            pltpu.VMEM(wave.shape, wave.dtype),
            pltpu.SemaphoreType.DMA((sectors, 3)),
        ],
        compiler_params=params(),
        cost_estimate=cost(4 * terms * sectors * width**3, 4 * left.size),
    )(kept, *in_hbm(wave, left, right))


def second_sums(kept, wave, sigma, left, right):
    terms, sectors, width, _ = left.shape
    return pl.pallas_call(
        second_kernel,
        in_specs=[smem()] + [vmem()] * 2 + [hbm()] * 2,
        out_specs=[vmem()] * 2,
        out_shape=[jax.ShapeDtypeStruct(wave.shape, jnp.float32)] * 2,
        scratch_shapes=[
            pltpu.VMEM(left.shape, left.dtype),
            pltpu.VMEM(right.shape, right.dtype),
            pltpu.SemaphoreType.DMA((sectors, 2)),
        ],
        compiler_params=params(),
        cost_estimate=cost(4 * terms * sectors * width**3, 4 * left.size),
    )(kept, wave, sigma, *in_hbm(left, right))


def gathered_sums(partial, kept):
    rows, width = partial.shape
    ways = lax.axis_size(NEAR)
    piece = lax.all_to_all(partial.reshape(ways, rows // ways, width), NEAR, 0, 0).sum(0)
    piece = piece + lax.ppermute(piece, "z1", SWAP)
    sector = lax.axis_index(NEAR) * kept.shape[1] // ways
    cols = jnp.arange(width, dtype=jnp.int32)
    piece = jnp.where(cols[None, :] < kept[0, sector], piece, 0.0)
    return lax.all_to_all(jnp.broadcast_to(piece[None], (ways,) + piece.shape), NEAR, 0, 0).reshape(rows, width)


def shards(wave_in, kept, left_ops, right_ops):
    _, sectors, width, _ = wave_in.shape
    core = lax.axis_index("core")
    wave = wave_in.reshape(sectors * width, width)
    like = jax.ShapeDtypeStruct(wave.shape, jnp.float32)

    left, right = left_ops[0], right_ops[0]
    sums = first_sums(kept, wave, left, right)
    sums, state = second_sums(kept, wave, gathered_sums(sums, kept), left, right)
    wave_out = pl.pallas_call(
        own_kernel,
        in_specs=[vmem()] * 2,
        out_specs=vmem(),
        out_shape=like,
        compiler_params=params(),
        cost_estimate=cost(12 * wave.size, 12 * wave.size),
    )(state, gathered_sums(sums, kept))
    far = lax.ppermute(wave_out, SEC + ("z1", "z0"), mirrored())
    near = lax.ppermute(wave_out, "core", SWAP)
    bound = pl.pallas_call(
        functools.partial(bound_kernel, sectors),
        in_specs=[smem()] + [vmem()] * 3,
        out_specs=vmem(),
        out_shape=like,
        compiler_params=params(),
        cost_estimate=cost(12 * sectors * width**3, 16 * wave.size),
    )(core.astype(jnp.int32).reshape(1, 1), wave_out, near, far)
    return (wave_out.reshape(wave_in.shape), bound.reshape(wave_in.shape))


def solution(mesh):
    split = Mesh(mesh.devices.reshape(2, 2, 2, 2, 4, 4), SEC + OP)
    return jax.shard_map(
        shards,
        mesh=split,
        in_specs=(
            P(SEC, None, None, None),
            P(SEC, None),
            P(SEC, OP, None, None, None),
            P(SEC, OP, None, None, None),
        ),
        out_specs=(P(SEC, None, None, None), P(SEC, None, None, None)),
        check_vma=False,
    )
```

```python
import math

import jax
import jax.numpy as jnp
from jax import lax
from jax.experimental import pallas as pl
from jax.experimental.pallas import tpu as pltpu
from jax.sharding import Mesh, PartitionSpec as P

EPS = 1e-06
STEP_COEF = 0.5
SEC = ("zh", "core")
OP = ("z1", "z0", "y", "x")
NEAR = ("z0", "y", "x")
SWAP = [(0, 1), (1, 0)]
VMEM_LIMIT = 24 * 2**20
CHUNK = 32


def mirrored():
    pairs = []
    for z in range(8):
        far = 7 - z
        pairs.append(((z // 4 * 2 + 1) * 4 + z % 4, (far // 4 * 2) * 4 + far % 4))
    return pairs


def masked(block, kept):
    cols = lax.broadcasted_iota(jnp.int32, block.shape, block.ndim - 1)
    return jnp.where(cols < kept, block, 0.0)


def folded(block):
    return block.reshape(-1, 8, block.shape[-1]).sum(0)


def chunk(i):
    return pl.ds(pl.multiple_of(i * CHUNK, CHUNK), CHUNK)


def update(rows, width, read_state, read_sigma, out_ref):
    count = rows // CHUNK
    zero = jnp.zeros((8, width), jnp.float32)

    def products(i, sums):
        state = read_state(i)
        return sums[0] + folded(state * state), sums[1] + folded(state * read_sigma(i))

    pp, ps = lax.fori_loop(0, count, products, (zero, zero), unroll=4)
    theta = jnp.sum(ps) / (jnp.sum(pp) + EPS)

    def trials(i, total):
        trial = (1.0 + STEP_COEF * theta) * read_state(i) - STEP_COEF * read_sigma(i)
        out_ref[chunk(i), :] = trial
        return total + folded(trial * trial)

    tt = lax.fori_loop(0, count, trials, zero, unroll=4)
    scale = lax.rsqrt(jnp.sum(tt) / (rows * width) + EPS)

    def scaled(i, carry):
        out_ref[chunk(i), :] = out_ref[chunk(i), :] * scale
        return carry

    lax.fori_loop(0, count, scaled, 0, unroll=4)


def sector_sums(state, left_ref, right_ref, s):
    terms = left_ref.shape[0]
    right = jnp.concatenate([right_ref[k, s] for k in range(terms)], axis=1)
    mixed = jnp.dot(state.astype(jnp.bfloat16), right, preferred_element_type=jnp.float32).astype(jnp.bfloat16)
    width = state.shape[1]
    mixed = jnp.concatenate([mixed[:, k * width : (k + 1) * width] for k in range(terms)], axis=0)
    left = jnp.concatenate([left_ref[k, s] for k in range(terms)], axis=1)
    return jnp.dot(left, mixed, preferred_element_type=jnp.float32)


def fetch(copies):
    started = []
    for s, (pairs, sems) in enumerate(copies):
        started.append([pltpu.make_async_copy(source, target, sems.at[j]) for j, (source, target) in enumerate(pairs)])
        for copy in started[s]:
            copy.start()
    return started


def first_kernel(kept_ref, wave_hbm, left_hbm, right_hbm, out_ref, left_ref, right_ref, wave_ref, sems):
    sectors, width = kept_ref.shape[1], wave_ref.shape[1]
    parts = [pl.ds(s * width, width) for s in range(sectors)]
    copies = fetch(
        [
            (
                [
                    (wave_hbm.at[parts[s]], wave_ref.at[parts[s]]),
                    (right_hbm.at[:, s], right_ref.at[:, s]),
                    (left_hbm.at[:, s], left_ref.at[:, s]),
                ],
                sems.at[s],
            )
            for s in range(sectors)
        ]
    )
    for s in range(sectors):
        for copy in copies[s]:
            copy.wait()
        out_ref[parts[s], :] = sector_sums(masked(wave_ref[parts[s], :], kept_ref[0, s]), left_ref, right_ref, s)


def second_kernel(kept_ref, wave_ref, sigma_ref, left_hbm, right_hbm, out_ref, state_ref, left_ref, right_ref, sems):
    sectors = kept_ref.shape[1]
    rows, width = wave_ref.shape
    share = rows // CHUNK // sectors
    copies = fetch(
        [
            (
                [(right_hbm.at[:, s], right_ref.at[:, s]), (left_hbm.at[:, s], left_ref.at[:, s])],
                sems.at[s],
            )
            for s in range(sectors)
        ]
    )
    update(
        rows,
        width,
        lambda i: masked(wave_ref[chunk(i), :], kept_ref[0, i // share]),
        lambda i: sigma_ref[chunk(i), :],
        state_ref,
    )
    for s in range(sectors):
        part = pl.ds(s * width, width)
        for copy in copies[s]:
            copy.wait()
        out_ref[part, :] = sector_sums(state_ref[part, :], left_ref, right_ref, s)


def own_kernel(state_ref, sigma_ref, out_ref):
    rows, width = state_ref.shape
    update(rows, width, lambda i: state_ref[chunk(i), :], lambda i: sigma_ref[chunk(i), :], out_ref)


def bound_kernel(place_ref, wave_ref, near_ref, *refs):
    sectors = len(refs) - 4
    far_refs, (wave_out, bound_out, bound_ref, sems) = refs[:sectors], refs[sectors:]
    width = wave_ref.shape[1]
    leaving = pltpu.make_async_copy(wave_ref, wave_out, sems.at[sectors])
    leaving.start()
    even = place_ref[0, 0] == 0
    copies = []
    for k in range(sectors):
        rows = pl.ds(pl.multiple_of((place_ref[0, 1] ^ k) * width, width), width)
        near = near_ref[rows, :]
        partner = near + jnp.where(even, far_refs[k][...], near)
        bound_ref[rows, :] = lax.dot_general(
            wave_ref[rows, :],
            partner,
            (((0,), (0,)), ((), ())),
            precision=lax.Precision.HIGHEST,
            preferred_element_type=jnp.float32,
        ) / math.sqrt(width)
        copies.append(pltpu.make_async_copy(bound_ref.at[rows], bound_out.at[rows], sems.at[k]))
        copies[k].start()
    for copy in copies:
        copy.wait()
    leaving.wait()


def params():
    return pltpu.CompilerParams(vmem_limit_bytes=VMEM_LIMIT)


def cost(flops, transfer):
    return pl.CostEstimate(flops=flops, bytes_accessed=transfer, transcendentals=0)


def smem():
    return pl.BlockSpec(memory_space=pltpu.SMEM)


def vmem():
    return pl.BlockSpec(memory_space=pltpu.VMEM)


def hbm():
    return pl.BlockSpec(memory_space=pltpu.HBM)


def in_hbm(*arrays):
    return [pltpu.with_memory_space_constraint(array, pltpu.HBM) for array in arrays]


def first_sums(kept, wave, left, right):
    terms, sectors, width, _ = left.shape
    return pl.pallas_call(
        first_kernel,
        in_specs=[smem()] + [hbm()] * 3,
        out_specs=vmem(),
        out_shape=jax.ShapeDtypeStruct(wave.shape, jnp.float32),
        scratch_shapes=[
            pltpu.VMEM(left.shape, left.dtype),
            pltpu.VMEM(right.shape, right.dtype),
            pltpu.VMEM(wave.shape, wave.dtype),
            pltpu.SemaphoreType.DMA((sectors, 3)),
        ],
        compiler_params=params(),
        cost_estimate=cost(4 * terms * sectors * width**3, 4 * left.size),
    )(kept, *in_hbm(wave, left, right))


def second_sums(kept, wave, sigma, left, right):
    terms, sectors, width, _ = left.shape
    return pl.pallas_call(
        second_kernel,
        in_specs=[smem()] + [vmem()] * 2 + [hbm()] * 2,
        out_specs=[vmem()] * 2,
        out_shape=[jax.ShapeDtypeStruct(wave.shape, jnp.float32)] * 2,
        scratch_shapes=[
            pltpu.VMEM(left.shape, left.dtype),
            pltpu.VMEM(right.shape, right.dtype),
            pltpu.SemaphoreType.DMA((sectors, 2)),
        ],
        compiler_params=params(),
        cost_estimate=cost(4 * terms * sectors * width**3, 4 * left.size),
    )(kept, wave, sigma, *in_hbm(left, right))


def gathered_sums(partial, kept):
    rows, width = partial.shape
    ways = lax.axis_size(NEAR)
    piece = lax.all_to_all(partial.reshape(ways, rows // ways, width), NEAR, 0, 0).sum(0)
    piece = piece + lax.ppermute(piece, "z1", SWAP)
    sector = lax.axis_index(NEAR) * kept.shape[1] // ways
    cols = jnp.arange(width, dtype=jnp.int32)
    piece = jnp.where(cols[None, :] < kept[0, sector], piece, 0.0)
    return lax.all_to_all(jnp.broadcast_to(piece[None], (ways,) + piece.shape), NEAR, 0, 0).reshape(rows, width)


def shards(wave_in, kept, left_ops, right_ops):
    _, sectors, width, _ = wave_in.shape
    wave = wave_in.reshape(sectors * width, width)
    like = jax.ShapeDtypeStruct(wave.shape, jnp.float32)

    left, right = left_ops[0], right_ops[0]
    sums = first_sums(kept, wave, left, right)
    sums, state = second_sums(kept, wave, gathered_sums(sums, kept), left, right)
    wave_out = pl.pallas_call(
        own_kernel,
        in_specs=[vmem()] * 2,
        out_specs=vmem(),
        out_shape=like,
        compiler_params=params(),
        cost_estimate=cost(12 * wave.size, 12 * wave.size),
    )(state, gathered_sums(sums, kept))
    near = lax.ppermute(wave_out, "core", SWAP)
    y = lax.axis_index("y")
    far = [lax.ppermute(lax.dynamic_slice_in_dim(wave_out, y * width, width), SEC + ("z1", "z0"), mirrored())]
    for k in range(1, sectors):
        far.append(lax.ppermute(far[0], ("core", "y"), [(i, i ^ k) for i in range(sectors)]))
    place = jnp.stack([lax.axis_index("core"), y]).astype(jnp.int32).reshape(1, 2)
    wave_out, bound = pl.pallas_call(
        bound_kernel,
        in_specs=[smem()] + [vmem()] * (2 + sectors),
        out_specs=[hbm()] * 2,
        out_shape=[like] * 2,
        scratch_shapes=[pltpu.VMEM(wave.shape, jnp.float32), pltpu.SemaphoreType.DMA((sectors + 1,))],
        compiler_params=params(),
        cost_estimate=cost(12 * sectors * width**3, 16 * wave.size),
    )(place, wave_out, near, *far)
    return (wave_out.reshape(wave_in.shape), bound.reshape(wave_in.shape))


def solution(mesh):
    split = Mesh(mesh.devices.reshape(2, 2, 2, 2, 4, 4), SEC + OP)
    return jax.shard_map(
        shards,
        mesh=split,
        in_specs=(
            P(SEC, None, None, None),
            P(SEC, None),
            P(SEC, OP, None, None, None),
            P(SEC, OP, None, None, None),
        ),
        out_specs=(P(SEC, None, None, None), P(SEC, None, None, None)),
        check_vma=False,
    )
```

```python
import math

import jax
import jax.numpy as jnp
from jax import lax
from jax.experimental import pallas as pl
from jax.experimental.pallas import tpu as pltpu
from jax.sharding import Mesh, PartitionSpec as P

EPS = 1e-06
STEP_COEF = 0.5
SEC = ("zh", "core")
OP = ("z1", "z0", "y", "x")
NEAR = ("z0", "y", "x")
SWAP = [(0, 1), (1, 0)]
VMEM_LIMIT = 24 * 2**20
CHUNK = 32


def mirrored():
    pairs = []
    for z in range(8):
        far = 7 - z
        pairs.append(((z // 4 * 2 + 1) * 4 + z % 4, (far // 4 * 2) * 4 + far % 4))
    return pairs


def spread(mask, rows):
    return jnp.concatenate([mask] * (rows // mask.shape[0]), axis=0)


def folded(block):
    return block.reshape(-1, 8, block.shape[-1]).sum(0)


def chunk(i):
    return pl.ds(pl.multiple_of(i * CHUNK, CHUNK), CHUNK)


def update(rows, width, read_state, read_sigma, out_ref):
    count = rows // CHUNK
    zero = jnp.zeros((8, width), jnp.float32)

    def products(i, sums):
        state = read_state(i)
        return sums[0] + folded(state * state), sums[1] + folded(state * read_sigma(i))

    pp, ps = lax.fori_loop(0, count, products, (zero, zero), unroll=4)
    theta = jnp.sum(ps) / (jnp.sum(pp) + EPS)

    def trials(i, total):
        trial = (1.0 + STEP_COEF * theta) * read_state(i) - STEP_COEF * read_sigma(i)
        out_ref[chunk(i), :] = trial
        return total + folded(trial * trial)

    tt = lax.fori_loop(0, count, trials, zero, unroll=4)
    scale = lax.rsqrt(jnp.sum(tt) / (rows * width) + EPS)

    def scaled(i, carry):
        out_ref[chunk(i), :] = out_ref[chunk(i), :] * scale
        return carry

    lax.fori_loop(0, count, scaled, 0, unroll=4)


def sector_sums(state, left_ref, right_ref, s):
    terms = left_ref.shape[0]
    right = jnp.concatenate([right_ref[k, s] for k in range(terms)], axis=1)
    mixed = jnp.dot(state.astype(jnp.bfloat16), right, preferred_element_type=jnp.float32).astype(jnp.bfloat16)
    width = state.shape[1]
    mixed = jnp.concatenate([mixed[:, k * width : (k + 1) * width] for k in range(terms)], axis=0)
    left = jnp.concatenate([left_ref[k, s] for k in range(terms)], axis=1)
    return jnp.dot(left, mixed, preferred_element_type=jnp.float32)


def fetch(copies):
    started = []
    for s, (pairs, sems) in enumerate(copies):
        started.append([pltpu.make_async_copy(source, target, sems.at[j]) for j, (source, target) in enumerate(pairs)])
        for copy in started[s]:
            copy.start()
    return started


def first_kernel(
    kept_hbm, wave_hbm, left_hbm, right_hbm, out_ref, state_ref, mask_ref, left_ref, right_ref, kept_ref, sems, kept_sem
):
    sectors, width = kept_ref.shape[1], state_ref.shape[1]
    kept_copy = pltpu.make_async_copy(kept_hbm, kept_ref, kept_sem)
    kept_copy.start()
    parts = [pl.ds(s * width, width) for s in range(sectors)]
    copies = fetch(
        [
            (
                [
                    (wave_hbm.at[parts[s]], state_ref.at[parts[s]]),
                    (right_hbm.at[:, s], right_ref.at[:, s]),
                    (left_hbm.at[:, s], left_ref.at[:, s]),
                ],
                sems.at[s],
            )
            for s in range(sectors)
        ]
    )
    kept_copy.wait()
    for s in range(sectors):
        cols = lax.broadcasted_iota(jnp.int32, mask_ref.shape[1:], 1)
        mask_ref[s] = jnp.where(cols < kept_ref[0, s], 1.0, 0.0)
    for s in range(sectors):
        for copy in copies[s]:
            copy.wait()
        state = spread(mask_ref[s], width) * state_ref[parts[s], :]
        state_ref[parts[s], :] = state
        out_ref[parts[s], :] = sector_sums(state, left_ref, right_ref, s)


def second_kernel(old_ref, sigma_ref, left_hbm, right_hbm, out_ref, state_ref, left_ref, right_ref, sems):
    rows, width = old_ref.shape
    sectors = rows // width
    copies = fetch(
        [
            (
                [(right_hbm.at[:, s], right_ref.at[:, s]), (left_hbm.at[:, s], left_ref.at[:, s])],
                sems.at[s],
            )
            for s in range(sectors)
        ]
    )
    update(rows, width, lambda i: old_ref[chunk(i), :], lambda i: sigma_ref[chunk(i), :], state_ref)
    for s in range(sectors):
        part = pl.ds(s * width, width)
        for copy in copies[s]:
            copy.wait()
        out_ref[part, :] = sector_sums(state_ref[part, :], left_ref, right_ref, s)


def own_kernel(state_ref, sigma_ref, out_ref):
    rows, width = state_ref.shape
    update(rows, width, lambda i: state_ref[chunk(i), :], lambda i: sigma_ref[chunk(i), :], out_ref)


def copies_kernel(here_ref, there_ref, mask_ref, out_ref):
    ways = out_ref.shape[0]
    sector = lax.axis_index(NEAR) * mask_ref.shape[0] // ways
    piece = spread(mask_ref[sector], here_ref.shape[0]) * (here_ref[...] + there_ref[...])
    for i in range(ways):
        out_ref[i] = piece


def halves(block):
    high = block.astype(jnp.bfloat16)
    return high, (block - high.astype(jnp.float32)).astype(jnp.bfloat16)


def near_kernel(wave_ref, near_ref, wave_out, product_ref, high_ref, low_ref, sem):
    leaving = pltpu.make_async_copy(wave_ref, wave_out, sem)
    leaving.start()
    rows, width = wave_ref.shape
    for s in range(rows // width):
        part = pl.ds(s * width, width)
        wave = wave_ref[part, :].T
        high_ref[part, :], low_ref[part, :] = halves(wave)
        product_ref[part, :] = jnp.dot(
            wave, near_ref[part, :], precision=lax.Precision.HIGHEST, preferred_element_type=jnp.float32
        )
    leaving.wait()


def bound_kernel(place_ref, product_ref, high_ref, low_ref, *refs):
    sectors = len(refs) - 3
    far_refs, (out_hbm, bound_ref, sems) = refs[:sectors], refs[sectors:]
    width = product_ref.shape[1]
    even = place_ref[0, 0] == 0
    copies = []
    for k in range(sectors):
        rows = pl.ds(pl.multiple_of((place_ref[0, 1] ^ k) * width, width), width)
        far_high, far_low = halves(far_refs[k][...])
        near = product_ref[rows, :]
        far = jnp.dot(high_ref[rows, :], far_high, preferred_element_type=jnp.float32)
        far += jnp.dot(high_ref[rows, :], far_low, preferred_element_type=jnp.float32)
        far += jnp.dot(low_ref[rows, :], far_high, preferred_element_type=jnp.float32)
        bound_ref[rows, :] = (near + jnp.where(even, far, near)) / math.sqrt(width)
        copies.append(pltpu.make_async_copy(bound_ref.at[rows], out_hbm.at[rows], sems.at[k]))
        if k % 2:
            copies[k - 1].start()
            copies[k].start()
    for copy in copies:
        copy.wait()


def params():
    return pltpu.CompilerParams(vmem_limit_bytes=VMEM_LIMIT)


def cost(flops, transfer):
    return pl.CostEstimate(flops=flops, bytes_accessed=transfer, transcendentals=0)


def smem():
    return pl.BlockSpec(memory_space=pltpu.SMEM)


def vmem():
    return pl.BlockSpec(memory_space=pltpu.VMEM)


def hbm():
    return pl.BlockSpec(memory_space=pltpu.HBM)


def in_hbm(*arrays):
    return [pltpu.with_memory_space_constraint(array, pltpu.HBM) for array in arrays]


def first_sums(kept, wave, left, right):
    terms, sectors, width, _ = left.shape
    return pl.pallas_call(
        first_kernel,
        in_specs=[hbm()] * 4,
        out_specs=[vmem()] * 3,
        out_shape=[jax.ShapeDtypeStruct(wave.shape, jnp.float32)] * 2
        + [jax.ShapeDtypeStruct((sectors, 8, width), jnp.float32)],
        scratch_shapes=[
            pltpu.VMEM(left.shape, left.dtype),
            pltpu.VMEM(right.shape, right.dtype),
            pltpu.SMEM(kept.shape, kept.dtype),
            pltpu.SemaphoreType.DMA((sectors, 3)),
            pltpu.SemaphoreType.DMA,
        ],
        compiler_params=params(),
        cost_estimate=cost(4 * terms * sectors * width**3, 4 * left.size),
    )(*in_hbm(kept, wave, left, right))


def second_sums(state, sigma, left, right):
    terms, sectors, width, _ = left.shape
    return pl.pallas_call(
        second_kernel,
        in_specs=[vmem()] * 2 + [hbm()] * 2,
        out_specs=[vmem()] * 2,
        out_shape=[jax.ShapeDtypeStruct(state.shape, jnp.float32)] * 2,
        scratch_shapes=[
            pltpu.VMEM(left.shape, left.dtype),
            pltpu.VMEM(right.shape, right.dtype),
            pltpu.SemaphoreType.DMA((sectors, 2)),
        ],
        compiler_params=params(),
        cost_estimate=cost(4 * terms * sectors * width**3, 4 * left.size),
    )(state, sigma, *in_hbm(left, right))


def gathered_sums(partial, mask):
    rows, width = partial.shape
    ways = lax.axis_size(NEAR)
    piece = lax.all_to_all(partial.reshape(ways, rows // ways, width), NEAR, 0, 0).sum(0)
    copies = pl.pallas_call(
        copies_kernel,
        in_specs=[vmem()] * 3,
        out_specs=vmem(),
        out_shape=jax.ShapeDtypeStruct((ways, rows // ways, width), jnp.float32),
        compiler_params=params(),
        cost_estimate=cost(2 * piece.size, 4 * partial.size),
    )(piece, lax.ppermute(piece, "z1", SWAP), mask)
    return lax.all_to_all(copies, NEAR, 0, 0).reshape(rows, width)


def shards(wave_in, kept, left_ops, right_ops):
    _, sectors, width, _ = wave_in.shape
    wave = wave_in.reshape(sectors * width, width)
    like = jax.ShapeDtypeStruct(wave.shape, jnp.float32)

    left, right = left_ops[0], right_ops[0]
    sums, state, mask = first_sums(kept, wave, left, right)
    sums, state = second_sums(state, gathered_sums(sums, mask), left, right)
    wave_out = pl.pallas_call(
        own_kernel,
        in_specs=[vmem()] * 2,
        out_specs=vmem(),
        out_shape=like,
        compiler_params=params(),
        cost_estimate=cost(12 * wave.size, 12 * wave.size),
    )(state, gathered_sums(sums, mask))
    near = lax.ppermute(wave_out, "core", SWAP)
    y = lax.axis_index("y")
    far = [lax.ppermute(lax.dynamic_slice_in_dim(wave_out, y * width, width), SEC + ("z1", "z0"), mirrored())]
    for k in range(1, sectors):
        far.append(lax.ppermute(far[0], ("core", "y"), [(i, i ^ k) for i in range(sectors)]))
    place = jnp.stack([lax.axis_index("core"), y]).astype(jnp.int32).reshape(1, 2)
    wave_out, *products = pl.pallas_call(
        near_kernel,
        in_specs=[vmem()] * 2,
        out_specs=[hbm()] + [vmem()] * 3,
        out_shape=[like, like] + [jax.ShapeDtypeStruct(wave.shape, jnp.bfloat16)] * 2,
        scratch_shapes=[pltpu.SemaphoreType.DMA],
        compiler_params=params(),
        cost_estimate=cost(12 * sectors * width**3, 16 * wave.size),
    )(wave_out, near)
    bound = pl.pallas_call(
        bound_kernel,
        in_specs=[smem()] + [vmem()] * (3 + sectors),
        out_specs=hbm(),
        out_shape=like,
        scratch_shapes=[pltpu.VMEM(wave.shape, jnp.float32), pltpu.SemaphoreType.DMA((sectors,))],
        compiler_params=params(),
        cost_estimate=cost(6 * sectors * width**3, 16 * wave.size),
    )(place, *products, *far)
    return (wave_out.reshape(wave_in.shape), bound.reshape(wave_in.shape))


def solution(mesh):
    split = Mesh(mesh.devices.reshape(2, 2, 2, 2, 4, 4), SEC + OP)
    return jax.shard_map(
        shards,
        mesh=split,
        in_specs=(
            P(SEC, None, None, None),
            P(SEC, None),
            P(SEC, OP, None, None, None),
            P(SEC, OP, None, None, None),
        ),
        out_specs=(P(SEC, None, None, None), P(SEC, None, None, None)),
        check_vma=False,
    )
```

```python
import math

import jax
import jax.numpy as jnp
from jax import lax
from jax.experimental import pallas as pl
from jax.experimental.pallas import tpu as pltpu
from jax.sharding import Mesh, PartitionSpec as P

EPS = 1e-06
STEP_COEF = 0.5
SEC = ("zh", "core")
OP = ("z1", "z0", "y", "x")
NEAR = ("z0", "y", "x")
SWAP = [(0, 1), (1, 0)]
VMEM_LIMIT = 24 * 2**20
CHUNK = 32


def across():
    pairs = []
    for z in range(8):
        far = z ^ 6
        pairs.append(((z // 4 * 2 + 1) * 4 + z % 4, (far // 4 * 2) * 4 + far % 4))
    return pairs


def spread(mask, rows):
    return jnp.concatenate([mask] * (rows // mask.shape[0]), axis=0)


def folded(block):
    return block.reshape(-1, 8, block.shape[-1]).sum(0)


def chunk(i):
    return pl.ds(pl.multiple_of(i * CHUNK, CHUNK), CHUNK)


def update(rows, width, read_state, read_sigma, out_ref):
    count = rows // CHUNK
    zero = jnp.zeros((8, width), jnp.float32)

    def products(i, sums):
        state = read_state(i)
        return sums[0] + folded(state * state), sums[1] + folded(state * read_sigma(i))

    pp, ps = lax.fori_loop(0, count, products, (zero, zero), unroll=4)
    theta = jnp.sum(ps) / (jnp.sum(pp) + EPS)

    def trials(i, total):
        trial = (1.0 + STEP_COEF * theta) * read_state(i) - STEP_COEF * read_sigma(i)
        out_ref[chunk(i), :] = trial
        return total + folded(trial * trial)

    tt = lax.fori_loop(0, count, trials, zero, unroll=4)
    scale = lax.rsqrt(jnp.sum(tt) / (rows * width) + EPS)

    def scaled(i, carry):
        out_ref[chunk(i), :] = out_ref[chunk(i), :] * scale
        return carry

    lax.fori_loop(0, count, scaled, 0, unroll=4)


def sector_sums(state, left_ref, right_ref, s):
    terms = left_ref.shape[0]
    right = jnp.concatenate([right_ref[k, s] for k in range(terms)], axis=1)
    mixed = jnp.dot(state.astype(jnp.bfloat16), right, preferred_element_type=jnp.float32).astype(jnp.bfloat16)
    width = state.shape[1]
    mixed = jnp.concatenate([mixed[:, k * width : (k + 1) * width] for k in range(terms)], axis=0)
    left = jnp.concatenate([left_ref[k, s] for k in range(terms)], axis=1)
    return jnp.dot(left, mixed, preferred_element_type=jnp.float32)


def fetch(copies):
    started = []
    for s, (pairs, sems) in enumerate(copies):
        started.append([pltpu.make_async_copy(source, target, sems.at[j]) for j, (source, target) in enumerate(pairs)])
        for copy in started[s]:
            copy.start()
    return started


def first_kernel(
    kept_hbm, wave_hbm, left_hbm, right_hbm, out_ref, state_ref, mask_ref, left_ref, right_ref, kept_ref, sems, kept_sem
):
    sectors, width = kept_ref.shape[1], state_ref.shape[1]
    kept_copy = pltpu.make_async_copy(kept_hbm, kept_ref, kept_sem)
    kept_copy.start()
    parts = [pl.ds(s * width, width) for s in range(sectors)]
    copies = fetch(
        [
            (
                [
                    (wave_hbm.at[parts[s]], state_ref.at[parts[s]]),
                    (right_hbm.at[:, s], right_ref.at[:, s]),
                    (left_hbm.at[:, s], left_ref.at[:, s]),
                ],
                sems.at[s],
            )
            for s in range(sectors)
        ]
    )
    kept_copy.wait()
    for s in range(sectors):
        cols = lax.broadcasted_iota(jnp.int32, mask_ref.shape[1:], 1)
        mask_ref[s] = jnp.where(cols < kept_ref[0, s], 1.0, 0.0)
    for s in range(sectors):
        for copy in copies[s]:
            copy.wait()
        state = spread(mask_ref[s], width) * state_ref[parts[s], :]
        state_ref[parts[s], :] = state
        out_ref[parts[s], :] = sector_sums(state, left_ref, right_ref, s)


def second_kernel(old_ref, sigma_ref, left_hbm, right_hbm, out_ref, state_ref, left_ref, right_ref, sems):
    rows, width = old_ref.shape
    sectors = rows // width
    copies = fetch(
        [
            (
                [(right_hbm.at[:, s], right_ref.at[:, s]), (left_hbm.at[:, s], left_ref.at[:, s])],
                sems.at[s],
            )
            for s in range(sectors)
        ]
    )
    update(rows, width, lambda i: old_ref[chunk(i), :], lambda i: sigma_ref[chunk(i), :], state_ref)
    for s in range(sectors):
        part = pl.ds(s * width, width)
        for copy in copies[s]:
            copy.wait()
        out_ref[part, :] = sector_sums(state_ref[part, :], left_ref, right_ref, s)


def own_kernel(state_ref, sigma_ref, out_ref):
    rows, width = state_ref.shape
    update(rows, width, lambda i: state_ref[chunk(i), :], lambda i: sigma_ref[chunk(i), :], out_ref)


def copies_kernel(here_ref, there_ref, mask_ref, out_ref):
    ways = out_ref.shape[0]
    sector = lax.axis_index(NEAR) * mask_ref.shape[0] // ways
    piece = spread(mask_ref[sector], here_ref.shape[0]) * (here_ref[...] + there_ref[...])
    for i in range(ways):
        out_ref[i] = piece


def halves(block):
    high = block.astype(jnp.bfloat16)
    return high, (block - high.astype(jnp.float32)).astype(jnp.bfloat16)


def near_kernel(wave_ref, near_ref, wave_out, product_ref, high_ref, low_ref, sem):
    leaving = pltpu.make_async_copy(wave_ref, wave_out, sem)
    leaving.start()
    rows, width = wave_ref.shape
    for s in range(rows // width):
        part = pl.ds(s * width, width)
        wave = wave_ref[part, :].T
        high_ref[part, :], low_ref[part, :] = halves(wave)
        product_ref[part, :] = jnp.dot(
            wave, near_ref[part, :], precision=lax.Precision.HIGHEST, preferred_element_type=jnp.float32
        )
    leaving.wait()


def bound_kernel(place_ref, product_ref, high_ref, low_ref, *refs):
    sectors = len(refs) - 3
    far_refs, (out_hbm, bound_ref, sems) = refs[:sectors], refs[sectors:]
    width = product_ref.shape[1]
    even = place_ref[0, 0] == 0
    copies = []
    for k in range(sectors):
        rows = pl.ds(pl.multiple_of((place_ref[0, 1] ^ k) * width, width), width)
        far_high, far_low = halves(far_refs[k][...])
        near = product_ref[rows, :]
        far = jnp.dot(high_ref[rows, :], far_high, preferred_element_type=jnp.float32)
        far += jnp.dot(high_ref[rows, :], far_low, preferred_element_type=jnp.float32)
        far += jnp.dot(low_ref[rows, :], far_high, preferred_element_type=jnp.float32)
        bound_ref[rows, :] = (near + jnp.where(even, far, near)) / math.sqrt(width)
        copies.append(pltpu.make_async_copy(bound_ref.at[rows], out_hbm.at[rows], sems.at[k]))
        if k % 2:
            copies[k - 1].start()
            copies[k].start()
    for copy in copies:
        copy.wait()


def params():
    return pltpu.CompilerParams(vmem_limit_bytes=VMEM_LIMIT)


def cost(flops, transfer):
    return pl.CostEstimate(flops=flops, bytes_accessed=transfer, transcendentals=0)


def smem():
    return pl.BlockSpec(memory_space=pltpu.SMEM)


def vmem():
    return pl.BlockSpec(memory_space=pltpu.VMEM)


def hbm():
    return pl.BlockSpec(memory_space=pltpu.HBM)


def in_hbm(*arrays):
    return [pltpu.with_memory_space_constraint(array, pltpu.HBM) for array in arrays]


def first_sums(kept, wave, left, right):
    terms, sectors, width, _ = left.shape
    return pl.pallas_call(
        first_kernel,
        in_specs=[hbm()] * 4,
        out_specs=[vmem()] * 3,
        out_shape=[jax.ShapeDtypeStruct(wave.shape, jnp.float32)] * 2
        + [jax.ShapeDtypeStruct((sectors, 8, width), jnp.float32)],
        scratch_shapes=[
            pltpu.VMEM(left.shape, left.dtype),
            pltpu.VMEM(right.shape, right.dtype),
            pltpu.SMEM(kept.shape, kept.dtype),
            pltpu.SemaphoreType.DMA((sectors, 3)),
            pltpu.SemaphoreType.DMA,
        ],
        compiler_params=params(),
        cost_estimate=cost(4 * terms * sectors * width**3, 4 * left.size),
    )(*in_hbm(kept, wave, left, right))


def second_sums(state, sigma, left, right):
    terms, sectors, width, _ = left.shape
    return pl.pallas_call(
        second_kernel,
        in_specs=[vmem()] * 2 + [hbm()] * 2,
        out_specs=[vmem()] * 2,
        out_shape=[jax.ShapeDtypeStruct(state.shape, jnp.float32)] * 2,
        scratch_shapes=[
            pltpu.VMEM(left.shape, left.dtype),
            pltpu.VMEM(right.shape, right.dtype),
            pltpu.SemaphoreType.DMA((sectors, 2)),
        ],
        compiler_params=params(),
        cost_estimate=cost(4 * terms * sectors * width**3, 4 * left.size),
    )(state, sigma, *in_hbm(left, right))


def gathered_sums(partial, mask):
    rows, width = partial.shape
    ways = lax.axis_size(NEAR)
    piece = lax.all_to_all(partial.reshape(ways, rows // ways, width), NEAR, 0, 0).sum(0)
    copies = pl.pallas_call(
        copies_kernel,
        in_specs=[vmem()] * 3,
        out_specs=vmem(),
        out_shape=jax.ShapeDtypeStruct((ways, rows // ways, width), jnp.float32),
        compiler_params=params(),
        cost_estimate=cost(2 * piece.size, 4 * partial.size),
    )(piece, lax.ppermute(piece, "z1", SWAP), mask)
    return lax.all_to_all(copies, NEAR, 0, 0).reshape(rows, width)


def shards(wave_in, kept, left_ops, right_ops):
    _, sectors, width, _ = wave_in.shape
    wave = wave_in.reshape(sectors * width, width)
    like = jax.ShapeDtypeStruct(wave.shape, jnp.float32)

    left, right = left_ops[0], right_ops[0]
    sums, state, mask = first_sums(kept, wave, left, right)
    sums, state = second_sums(state, gathered_sums(sums, mask), left, right)
    wave_out = pl.pallas_call(
        own_kernel,
        in_specs=[vmem()] * 2,
        out_specs=vmem(),
        out_shape=like,
        compiler_params=params(),
        cost_estimate=cost(12 * wave.size, 12 * wave.size),
    )(state, gathered_sums(sums, mask))
    near = lax.ppermute(wave_out, "core", SWAP)
    y = lax.axis_index("y")
    far = [lax.ppermute(lax.dynamic_slice_in_dim(wave_out, y * width, width), SEC + ("z1", "z0"), across())]
    for k in range(1, sectors):
        far.append(lax.ppermute(far[0], ("core", "y"), [(i, i ^ k) for i in range(sectors)]))
    place = jnp.stack([lax.axis_index("core"), y]).astype(jnp.int32).reshape(1, 2)
    wave_out, *products = pl.pallas_call(
        near_kernel,
        in_specs=[vmem()] * 2,
        out_specs=[hbm()] + [vmem()] * 3,
        out_shape=[like, like] + [jax.ShapeDtypeStruct(wave.shape, jnp.bfloat16)] * 2,
        scratch_shapes=[pltpu.SemaphoreType.DMA],
        compiler_params=params(),
        cost_estimate=cost(12 * sectors * width**3, 16 * wave.size),
    )(wave_out, near)
    bound = pl.pallas_call(
        bound_kernel,
        in_specs=[smem()] + [vmem()] * (3 + sectors),
        out_specs=hbm(),
        out_shape=like,
        scratch_shapes=[pltpu.VMEM(wave.shape, jnp.float32), pltpu.SemaphoreType.DMA((sectors,))],
        compiler_params=params(),
        cost_estimate=cost(6 * sectors * width**3, 16 * wave.size),
    )(place, *products, *far)
    return (wave_out.reshape(wave_in.shape), bound.reshape(wave_in.shape))


def solution(mesh):
    split = Mesh(mesh.devices.reshape(2, 2, 2, 2, 4, 4), SEC + OP)
    return jax.shard_map(
        shards,
        mesh=split,
        in_specs=(
            P(SEC, None, None, None),
            P(SEC, None),
            P(SEC, OP, None, None, None),
            P(SEC, OP, None, None, None),
        ),
        out_specs=(P(SEC, None, None, None), P(SEC, None, None, None)),
        check_vma=False,
    )
```

```python
import math

import jax
import jax.numpy as jnp
from jax import lax
from jax.experimental import pallas as pl
from jax.experimental.pallas import tpu as pltpu
from jax.sharding import Mesh, PartitionSpec as P

EPS = 1e-06
STEP_COEF = 0.5
SEC = ("zh", "core")
OP = ("z1", "z0", "y", "x")
NEAR = ("z0", "y", "x")
SWAP = [(0, 1), (1, 0)]
VMEM_LIMIT = 24 * 2**20
CHUNK = 32


def mirrored():
    pairs = []
    for z in range(8):
        far = 7 - z
        pairs.append(((z // 4 * 2 + 1) * 4 + z % 4, (far // 4 * 2) * 4 + far % 4))
    return pairs


def spread(mask, rows):
    return jnp.concatenate([mask] * (rows // mask.shape[0]), axis=0)


def folded(block):
    return block.reshape(-1, 8, block.shape[-1]).sum(0)


def chunk(i):
    return pl.ds(pl.multiple_of(i * CHUNK, CHUNK), CHUNK)


def update(rows, width, read_state, read_sigma, out_ref):
    count = rows // CHUNK
    zero = jnp.zeros((8, width), jnp.float32)

    def products(i, sums):
        state = read_state(i)
        return sums[0] + folded(state * state), sums[1] + folded(state * read_sigma(i))

    pp, ps = lax.fori_loop(0, count, products, (zero, zero), unroll=4)
    theta = jnp.sum(ps) / (jnp.sum(pp) + EPS)

    def trials(i, total):
        trial = (1.0 + STEP_COEF * theta) * read_state(i) - STEP_COEF * read_sigma(i)
        out_ref[chunk(i), :] = trial
        return total + folded(trial * trial)

    tt = lax.fori_loop(0, count, trials, zero, unroll=4)
    scale = lax.rsqrt(jnp.sum(tt) / (rows * width) + EPS)

    def scaled(i, carry):
        out_ref[chunk(i), :] = out_ref[chunk(i), :] * scale
        return carry

    lax.fori_loop(0, count, scaled, 0, unroll=4)


def sector_sums(state, left_ref, right_ref, s):
    terms = left_ref.shape[0]
    right = jnp.concatenate([right_ref[k, s] for k in range(terms)], axis=1)
    mixed = jnp.dot(state.astype(jnp.bfloat16), right, preferred_element_type=jnp.float32).astype(jnp.bfloat16)
    width = state.shape[1]
    mixed = jnp.concatenate([mixed[:, k * width : (k + 1) * width] for k in range(terms)], axis=0)
    left = jnp.concatenate([left_ref[k, s] for k in range(terms)], axis=1)
    return jnp.dot(left, mixed, preferred_element_type=jnp.float32)


def fetch(copies):
    started = []
    for s, (pairs, sems) in enumerate(copies):
        started.append([pltpu.make_async_copy(source, target, sems.at[j]) for j, (source, target) in enumerate(pairs)])
        for copy in started[s]:
            copy.start()
    return started


def first_kernel(
    kept_hbm, wave_hbm, left_hbm, right_hbm, out_ref, state_ref, mask_ref, left_ref, right_ref, kept_ref, sems, kept_sem
):
    sectors, width = kept_ref.shape[1], state_ref.shape[1]
    kept_copy = pltpu.make_async_copy(kept_hbm, kept_ref, kept_sem)
    kept_copy.start()
    parts = [pl.ds(s * width, width) for s in range(sectors)]
    copies = fetch(
        [
            (
                [
                    (wave_hbm.at[parts[s]], state_ref.at[parts[s]]),
                    (right_hbm.at[:, s], right_ref.at[:, s]),
                    (left_hbm.at[:, s], left_ref.at[:, s]),
                ],
                sems.at[s],
            )
            for s in range(sectors)
        ]
    )
    kept_copy.wait()
    for s in range(sectors):
        cols = lax.broadcasted_iota(jnp.int32, mask_ref.shape[1:], 1)
        mask_ref[s] = jnp.where(cols < kept_ref[0, s], 1.0, 0.0)
    for s in range(sectors):
        for copy in copies[s]:
            copy.wait()
        state = spread(mask_ref[s], width) * state_ref[parts[s], :]
        state_ref[parts[s], :] = state
        out_ref[parts[s], :] = sector_sums(state, left_ref, right_ref, s)


def second_kernel(old_ref, sigma_ref, left_hbm, right_hbm, out_ref, state_ref, left_ref, right_ref, sems):
    rows, width = old_ref.shape
    sectors = rows // width
    copies = fetch(
        [
            (
                [(right_hbm.at[:, s], right_ref.at[:, s]), (left_hbm.at[:, s], left_ref.at[:, s])],
                sems.at[s],
            )
            for s in range(sectors)
        ]
    )
    update(rows, width, lambda i: old_ref[chunk(i), :], lambda i: sigma_ref[chunk(i), :], state_ref)
    for s in range(sectors):
        part = pl.ds(s * width, width)
        for copy in copies[s]:
            copy.wait()
        out_ref[part, :] = sector_sums(state_ref[part, :], left_ref, right_ref, s)


def own_kernel(state_ref, sigma_ref, out_ref):
    rows, width = state_ref.shape
    update(rows, width, lambda i: state_ref[chunk(i), :], lambda i: sigma_ref[chunk(i), :], out_ref)


def copies_kernel(here_ref, there_ref, mask_ref, out_ref):
    ways = out_ref.shape[0]
    sector = lax.axis_index(NEAR) * mask_ref.shape[0] // ways
    piece = spread(mask_ref[sector], here_ref.shape[0]) * (here_ref[...] + there_ref[...])
    for i in range(ways):
        out_ref[i] = piece


def halves(block):
    high = block.astype(jnp.bfloat16)
    return high, (block - high.astype(jnp.float32)).astype(jnp.bfloat16)


def far_product(rows, high_ref, low_ref, far):
    far_high, far_low = halves(far)
    total = jnp.dot(high_ref[rows, :], far_high, preferred_element_type=jnp.float32)
    total += jnp.dot(high_ref[rows, :], far_low, preferred_element_type=jnp.float32)
    return total + jnp.dot(low_ref[rows, :], far_high, preferred_element_type=jnp.float32)


def near_kernel(place_ref, wave_ref, near_ref, far_ref, wave_out, product_ref, high_ref, low_ref, sem):
    leaving = pltpu.make_async_copy(wave_ref, wave_out, sem)
    leaving.start()
    rows, width = wave_ref.shape
    for s in range(rows // width):
        part = pl.ds(s * width, width)
        wave = wave_ref[part, :].T
        high_ref[part, :], low_ref[part, :] = halves(wave)
        product_ref[part, :] = jnp.dot(
            wave, near_ref[part, :], precision=lax.Precision.HIGHEST, preferred_element_type=jnp.float32
        )
    rows = pl.ds(pl.multiple_of(place_ref[0, 1] * width, width), width)
    near = product_ref[rows, :]
    far = far_product(rows, high_ref, low_ref, far_ref[...])
    product_ref[rows, :] = (near + jnp.where(place_ref[0, 0] == 0, far, near)) / math.sqrt(width)
    leaving.wait()


def bound_kernel(place_ref, product_ref, high_ref, low_ref, *refs):
    sectors = len(refs) - 2
    far_refs, (out_hbm, bound_ref, sems) = refs[: sectors - 1], refs[sectors - 1 :]
    width = product_ref.shape[1]
    even = place_ref[0, 0] == 0
    copies = []
    for k in range(sectors):
        rows = pl.ds(pl.multiple_of((place_ref[0, 1] ^ k) * width, width), width)
        source = bound_ref if k else product_ref
        if k:
            near = product_ref[rows, :]
            far = far_product(rows, high_ref, low_ref, far_refs[k - 1][...])
            bound_ref[rows, :] = (near + jnp.where(even, far, near)) / math.sqrt(width)
        copies.append(pltpu.make_async_copy(source.at[rows], out_hbm.at[rows], sems.at[k]))
        copies[k].start()
    for copy in copies:
        copy.wait()


def params():
    return pltpu.CompilerParams(vmem_limit_bytes=VMEM_LIMIT)


def cost(flops, transfer):
    return pl.CostEstimate(flops=flops, bytes_accessed=transfer, transcendentals=0)


def smem():
    return pl.BlockSpec(memory_space=pltpu.SMEM)


def vmem():
    return pl.BlockSpec(memory_space=pltpu.VMEM)


def hbm():
    return pl.BlockSpec(memory_space=pltpu.HBM)


def in_hbm(*arrays):
    return [pltpu.with_memory_space_constraint(array, pltpu.HBM) for array in arrays]


def first_sums(kept, wave, left, right):
    terms, sectors, width, _ = left.shape
    return pl.pallas_call(
        first_kernel,
        in_specs=[hbm()] * 4,
        out_specs=[vmem()] * 3,
        out_shape=[jax.ShapeDtypeStruct(wave.shape, jnp.float32)] * 2
        + [jax.ShapeDtypeStruct((sectors, 8, width), jnp.float32)],
        scratch_shapes=[
            pltpu.VMEM(left.shape, left.dtype),
            pltpu.VMEM(right.shape, right.dtype),
            pltpu.SMEM(kept.shape, kept.dtype),
            pltpu.SemaphoreType.DMA((sectors, 3)),
            pltpu.SemaphoreType.DMA,
        ],
        compiler_params=params(),
        cost_estimate=cost(4 * terms * sectors * width**3, 4 * left.size),
    )(*in_hbm(kept, wave, left, right))


def second_sums(state, sigma, left, right):
    terms, sectors, width, _ = left.shape
    return pl.pallas_call(
        second_kernel,
        in_specs=[vmem()] * 2 + [hbm()] * 2,
        out_specs=[vmem()] * 2,
        out_shape=[jax.ShapeDtypeStruct(state.shape, jnp.float32)] * 2,
        scratch_shapes=[
            pltpu.VMEM(left.shape, left.dtype),
            pltpu.VMEM(right.shape, right.dtype),
            pltpu.SemaphoreType.DMA((sectors, 2)),
        ],
        compiler_params=params(),
        cost_estimate=cost(4 * terms * sectors * width**3, 4 * left.size),
    )(state, sigma, *in_hbm(left, right))


def gathered_sums(partial, mask):
    rows, width = partial.shape
    ways = lax.axis_size(NEAR)
    piece = lax.all_to_all(partial.reshape(ways, rows // ways, width), NEAR, 0, 0).sum(0)
    copies = pl.pallas_call(
        copies_kernel,
        in_specs=[vmem()] * 3,
        out_specs=vmem(),
        out_shape=jax.ShapeDtypeStruct((ways, rows // ways, width), jnp.float32),
        compiler_params=params(),
        cost_estimate=cost(2 * piece.size, 4 * partial.size),
    )(piece, lax.ppermute(piece, "z1", SWAP), mask)
    return lax.all_to_all(copies, NEAR, 0, 0).reshape(rows, width)


def shards(wave_in, kept, left_ops, right_ops):
    _, sectors, width, _ = wave_in.shape
    wave = wave_in.reshape(sectors * width, width)
    like = jax.ShapeDtypeStruct(wave.shape, jnp.float32)

    left, right = left_ops[0], right_ops[0]
    sums, state, mask = first_sums(kept, wave, left, right)
    sums, state = second_sums(state, gathered_sums(sums, mask), left, right)
    wave_out = pl.pallas_call(
        own_kernel,
        in_specs=[vmem()] * 2,
        out_specs=vmem(),
        out_shape=like,
        compiler_params=params(),
        cost_estimate=cost(12 * wave.size, 12 * wave.size),
    )(state, gathered_sums(sums, mask))
    near = lax.ppermute(wave_out, "core", SWAP)
    y = lax.axis_index("y")
    far = [lax.ppermute(lax.dynamic_slice_in_dim(wave_out, y * width, width), SEC + ("z1", "z0"), mirrored())]
    for k in range(1, sectors):
        far.append(lax.ppermute(far[0], ("core", "y"), [(i, i ^ k) for i in range(sectors)]))
    place = jnp.stack([lax.axis_index("core"), y]).astype(jnp.int32).reshape(1, 2)
    wave_out, *products = pl.pallas_call(
        near_kernel,
        in_specs=[smem()] + [vmem()] * 3,
        out_specs=[hbm()] + [vmem()] * 3,
        out_shape=[like, like] + [jax.ShapeDtypeStruct(wave.shape, jnp.bfloat16)] * 2,
        scratch_shapes=[pltpu.SemaphoreType.DMA],
        compiler_params=params(),
        cost_estimate=cost(12 * sectors * width**3, 16 * wave.size),
    )(place, wave_out, near, far[0])
    bound = pl.pallas_call(
        bound_kernel,
        in_specs=[smem()] + [vmem()] * (2 + sectors),
        out_specs=hbm(),
        out_shape=like,
        scratch_shapes=[pltpu.VMEM(wave.shape, jnp.float32), pltpu.SemaphoreType.DMA((sectors,))],
        compiler_params=params(),
        cost_estimate=cost(6 * sectors * width**3, 16 * wave.size),
    )(place, *products, *far[1:])
    return (wave_out.reshape(wave_in.shape), bound.reshape(wave_in.shape))


def solution(mesh):
    split = Mesh(mesh.devices.reshape(2, 2, 2, 2, 4, 4), SEC + OP)
    return jax.shard_map(
        shards,
        mesh=split,
        in_specs=(
            P(SEC, None, None, None),
            P(SEC, None),
            P(SEC, OP, None, None, None),
            P(SEC, OP, None, None, None),
        ),
        out_specs=(P(SEC, None, None, None), P(SEC, None, None, None)),
        check_vma=False,
    )
```
